256 devices in a mesh: lat: 8 (over x_lo, y), lon: 32 (over z, x_hi, core).
Axes of the slice: x: 4 (x_hi: 2, x_lo: 2; x = x_hi * 2 + x_lo), y: 4, z: 8, core: 2. Of those that a mesh axis runs over, the one named last changes fastest.
Arguments:
- queries: bfloat16 [128, 512, 768], P('lat', 'lon'), may hold values from -28 to 28
- key_vectors: bfloat16 [128, 512, 768], P('lat', 'lon'), may hold values from -6 to 6
- value_vectors: bfloat16 [128, 512, 768], P('lat', 'lon'), may hold values from -6 to 6
- grad_output: bfloat16 [128, 512, 1536], P('lat', 'lon'), may hold values from -6 to 6
- out_weight: bfloat16 [768, 1536], replicated, may hold values from -0.21875 to 0.21875
Outputs:
- grad_queries: bfloat16 [128, 512, 768], P('lat', 'lon')
- grad_keys: bfloat16 [128, 512, 768], P('lat', 'lon')
- grad_values: bfloat16 [128, 512, 768], P('lat', 'lon')
- grad_weight: float32 [768, 1536], replicated
The draws below stay inside these ranges and needn't reach their ends.
All inputs are finite; a program needn't handle non-finite values.
Results may differ from the reference program's by a relative error of at most 0.019.
Values may be sent and summed in bfloat16 or wider, within the bound.
No kernel may reach another device: no remote copies, remote signals or barrier semaphores. Data moves between devices by JAX's collectives and lax.ppermute only.
A program may use at most 128 MiB of HBM per device.

```python
import jax
import jax.numpy as jnp
from jax import lax

HEADS = 6
HEAD_DIM = 128
WIDTH = 1536
WIN = 13
NH = 128
NW = 512


def drawn_fields(key):
    field_shape = (NH, NW, HEADS * HEAD_DIM)
    key_field = jnp.clip(jax.random.normal(jax.random.fold_in(key, 106), field_shape, jnp.float32), -6.0, 6.0)
    query_field = jnp.clip(jax.random.normal(jax.random.fold_in(key, 107), field_shape, jnp.float32), -6.0, 6.0)
    return (query_field, key_field)


def draw_queries(key, part):
    return drawn_fields(key)[0].astype(jnp.bfloat16)


def draw_key_vectors(key, part):
    return drawn_fields(key)[1].astype(jnp.bfloat16)


def level_of(stream_key, extent, split, low, largest):
    def one(dim, shards_of):
        steps = jax.random.uniform(jax.random.fold_in(jax.random.fold_in(stream_key, 6), dim), (shards_of,), jnp.float32, low / len(split), largest / len(split))
        return jnp.repeat(jnp.exp(steps), extent[dim] // shards_of).reshape((-1,) + (1,) * (len(extent) - dim - 1))

    gain = one(*split[0])
    for cut in split[1:]:
        gain = gain * one(*cut)
    return gain


def scatter_about(key, extent, width, limit, split=(), kind=jnp.bfloat16):
    level = level_of(key, extent, split, -0.22, 0.18) if split else 1.0
    entries = jax.random.normal(key, extent, jnp.float32) * width * level
    return jnp.minimum(jnp.maximum(entries, -limit), limit).astype(kind)


def setup_inputs(seed: int = 0) -> dict:
    key_of = jax.random.split(jax.random.key(seed), 6)
    return {
        "queries": draw_queries(jax.random.fold_in(key_of[5], 71), 0),
        "key_vectors": draw_key_vectors(jax.random.fold_in(key_of[5], 71), 0),
        "value_vectors": scatter_about(key_of[2], (NH, NW, HEADS * HEAD_DIM), 1.0, 6.0, ((0, 8), (1, 32))),
        "grad_output": scatter_about(key_of[3], (NH, NW, WIDTH), 1.0, 6.0, ((0, 8), (1, 32))),
        "out_weight": scatter_about(key_of[4], (HEADS * HEAD_DIM, WIDTH), (HEADS * HEAD_DIM) ** -0.5, 0.21875),
    }


def window_of(field, win_start, win_reach):
    band_rows = lax.dynamic_slice_in_dim(field, win_start, WIN, 0).astype(jnp.float32)
    stacked = jnp.stack([jnp.roll(band_rows, win_reach - offset, axis=1) for offset in range(WIN)], axis=1)
    return stacked.reshape(WIN, WIN, NW, HEADS, HEAD_DIM)


def spread_back(part, win_reach):
    total = jnp.roll(part[:, 0], 0 - win_reach, axis=1)
    for offset in range(1, WIN):
        total = total + jnp.roll(part[:, offset], offset - win_reach, axis=1)
    return total.reshape(WIN, NW, HEADS * HEAD_DIM)


def reference(queries, key_vectors, value_vectors, grad_output, out_weight):
    win_reach = (WIN - 1) // 2
    q_scale = HEAD_DIM ** -0.5
    channels = HEADS * HEAD_DIM
    grad_attn = jnp.dot(grad_output.reshape(NH * NW, WIDTH), out_weight.T, preferred_element_type=jnp.float32)
    grad_attn = grad_attn.astype(jnp.bfloat16).reshape(NH, NW, channels)

    def row_step(totals, row_idx):
        acc_key, acc_value = totals
        win_start = jnp.clip(row_idx - win_reach, 0, NH - WIN).astype(jnp.int32)
        query_row = lax.dynamic_index_in_dim(queries, row_idx, 0, keepdims=False).astype(jnp.float32).reshape(NW, HEADS, HEAD_DIM)
        grad_row = lax.dynamic_index_in_dim(grad_attn, row_idx, 0, keepdims=False).astype(jnp.float32).reshape(NW, HEADS, HEAD_DIM)
        key_win = window_of(key_vectors, win_start, win_reach)
        value_win = window_of(value_vectors, win_start, win_reach)
        scores = jnp.einsum("whd,abwhd->whab", query_row, key_win) * q_scale
        row_max = jnp.max(scores, axis=(2, 3), keepdims=True)
        exponent = jnp.exp(scores - row_max)
        prob_f = exponent / jnp.sum(exponent, axis=(2, 3), keepdims=True)
        prob_b = lax.optimization_barrier(prob_f.astype(jnp.bfloat16)).astype(jnp.float32)
        attended = jnp.einsum("whab,abwhd->whd", prob_b, value_win).astype(jnp.bfloat16)
        grad_prob = jnp.einsum("whd,abwhd->whab", grad_row, value_win)
        delta = jnp.sum(prob_f * grad_prob, axis=(2, 3), keepdims=True)
        grad_score = prob_f * (grad_prob - delta) * q_scale
        grad_score = lax.optimization_barrier(grad_score.astype(jnp.bfloat16)).astype(jnp.float32)
        grad_query = jnp.einsum("whab,abwhd->whd", grad_score, key_win).astype(jnp.bfloat16)
        key_terms = spread_back(jnp.einsum("whab,whd->abwhd", grad_score, query_row), win_reach)
        value_terms = spread_back(jnp.einsum("whab,whd->abwhd", prob_b, grad_row), win_reach)
        acc_key = lax.dynamic_update_slice_in_dim(acc_key, lax.dynamic_slice_in_dim(acc_key, win_start, WIN, 0) + key_terms, win_start, 0)
        acc_value = lax.dynamic_update_slice_in_dim(acc_value, lax.dynamic_slice_in_dim(acc_value, win_start, WIN, 0) + value_terms, win_start, 0)
        return (acc_key, acc_value), (attended.reshape(NW, channels), grad_query.reshape(NW, channels))

    zero_grads = jnp.zeros((NH, NW, channels), jnp.float32)
    (acc_key, acc_value), (attended, grad_queries) = lax.scan(row_step, (zero_grads, zero_grads), jnp.arange(NH, dtype=jnp.int32))
    grad_weight = jnp.dot(attended.reshape(NH * NW, channels).T, grad_output.reshape(NH * NW, WIDTH), preferred_element_type=jnp.float32)
    return grad_queries, acc_key.astype(jnp.bfloat16), acc_value.astype(jnp.bfloat16), grad_weight
```

```python
import jax
import jax.numpy as jnp
import numpy as np
from jax import lax
from jax.experimental import pallas as pl
from jax.experimental.pallas import tpu as pltpu
from jax.sharding import Mesh, PartitionSpec as P

HEADS = 6
HEAD_DIM = 128
WIDTH = 1536
WIN = 13
REACH = 6
ROWS = 16
COLS = 16
CHANNELS = HEADS * HEAD_DIM
TOKENS = ROWS * COLS
EDGE = REACH * COLS
SPAN = ROWS + 2 * REACH
MID = SPAN * COLS
SIDE = SPAN * REACH
SIDE_PAD = 176
TILES = 2
TILE_Q = TOKENS // TILES
MID_TILE = 320
SIDE_TILE = 128
KEYS = MID_TILE + 2 * SIDE_TILE
MID_STARTS = (0, 128)
SIDE_STARTS = (0, 48)
SCALE = HEAD_DIM ** -0.5
LAT = ("xl", "y")
LON = ("z", "xh", "core")
PLANE = ("xl", "y", "xh")
F32 = jnp.float32
BF16 = jnp.bfloat16


def key_places():
    mid_rows, mid_cols = np.divmod(np.arange(MID), COLS)
    side_rows, side_cols = np.divmod(np.arange(SIDE_PAD), REACH)
    unused = np.arange(SIDE_PAD) >= SIDE
    west_cols = np.where(unused, 1000, side_cols - REACH)
    east_cols = np.where(unused, 1000, side_cols + COLS)
    rows, cols = [], []
    for mid, side in zip(MID_STARTS, SIDE_STARTS):
        mids, sides = slice(mid, mid + MID_TILE), slice(side, side + SIDE_TILE)
        rows.append(np.concatenate([mid_rows[mids], side_rows[sides], side_rows[sides]]) - REACH)
        cols.append(np.concatenate([mid_cols[mids], west_cols[sides], east_cols[sides]]))
    return np.stack(rows), np.stack(cols)


def window_bias(first_row, total_rows):
    rows, cols = key_places()
    query_rows, query_cols = np.divmod(np.arange(TOKENS).reshape(TILES, TILE_Q), COLS)
    start = jnp.clip(first_row + query_rows - REACH, 0, total_rows - WIN)[:, None, :]
    key_rows = (first_row + rows)[:, :, None]
    near = np.abs(cols[:, :, None] - query_cols[:, None, :]) <= REACH
    keep = (key_rows >= start) & (key_rows < start + WIN) & near
    return jnp.where(keep, 0.0, -1e30).astype(F32)


def tile_keys(tile, own, edges, west, east):
    side = slice(SIDE_STARTS[tile], SIDE_STARTS[tile] + SIDE_TILE)
    if tile == 0:
        mid = [edges[0], own[: MID_TILE - EDGE]]
    else:
        mid = [own[TOKENS - (MID_TILE - EDGE) :], edges[1]]
    return jnp.concatenate(mid + [west[side], east[side]], axis=0)


def dot(a, b, dims):
    return lax.dot_general(a, b, (dims, ((), ())), preferred_element_type=F32)


def forward_kernel(q_ref, k_ref, v_ref, north_ref, south_ref, west_ref, east_ref, bias_ref, out_ref, lse_ref):
    keys = (k_ref[...], (north_ref[0], south_ref[0]), west_ref[0], east_ref[0])
    values = (v_ref[...], (north_ref[1], south_ref[1]), west_ref[1], east_ref[1])
    for tile in range(TILES):
        span = slice(tile * TILE_Q, (tile + 1) * TILE_Q)
        scores = dot(tile_keys(tile, *keys), q_ref[span, :], ((1,), (1,))) * SCALE + bias_ref[tile]
        top = jnp.max(scores, axis=0, keepdims=True)
        exponent = jnp.exp(scores - top)
        total = jnp.sum(exponent, axis=0, keepdims=True)
        prob = (exponent * (1.0 / total)).astype(BF16)
        attended = dot(prob, tile_keys(tile, *values), ((0,), (0,)))
        out_ref[span, :] = attended.astype(BF16)
        lse_ref[0, tile : tile + 1, :] = top + jnp.log(total)


def backward_kernel(
    q_ref, k_ref, v_ref, north_ref, south_ref, west_ref, east_ref, bias_ref, g_ref, lse_ref,
    dq_ref, mid_ref, dwest_ref, deast_ref, prob_s, score_s,
):
    @pl.when(pl.program_id(0) == 0)
    def _():
        prob_s[...] = jnp.zeros_like(prob_s)
        score_s[...] = jnp.zeros_like(score_s)

    keys = (k_ref[...], (north_ref[0], south_ref[0]), west_ref[0], east_ref[0])
    values = (v_ref[...], (north_ref[1], south_ref[1]), west_ref[1], east_ref[1])
    for tile in range(TILES):
        span = slice(tile * TILE_Q, (tile + 1) * TILE_Q)
        key_tile = tile_keys(tile, *keys)
        scores = dot(key_tile, q_ref[span, :], ((1,), (1,))) * SCALE + bias_ref[tile]
        prob = jnp.exp(scores - lse_ref[0, tile : tile + 1, :])
        grad_prob = dot(tile_keys(tile, *values), g_ref[span, :], ((1,), (1,)))
        delta = jnp.sum(prob * grad_prob, axis=0, keepdims=True)
        grad_score = (prob * (grad_prob - delta) * SCALE).astype(BF16)
        dq_ref[span, :] = dot(grad_score, key_tile, ((0,), (0,))).astype(BF16)
        mid, side = MID_STARTS[tile], SIDE_STARTS[tile]
        for part, scratch in ((prob.astype(BF16), prob_s), (grad_score, score_s)):
            scratch[mid : mid + MID_TILE, span] = part[:MID_TILE]
            for at, low in ((MID, MID_TILE), (MID + SIDE_PAD, MID_TILE + SIDE_TILE)):
                scratch[at + side : at + side + SIDE_TILE, span] = part[low : low + SIDE_TILE]
    for slot, scratch, other in ((0, score_s, q_ref), (1, prob_s, g_ref)):
        grads = dot(scratch[...], other[...], ((1,), (0,)))
        mid_ref[slot] = grads[:MID]
        dwest_ref[slot] = grads[MID : MID + SIDE_PAD].astype(BF16)
        deast_ref[slot] = grads[MID + SIDE_PAD :].astype(BF16)


def head_specs():
    tokens = pl.BlockSpec((TOKENS, HEAD_DIM), lambda h: (0, h))
    edge = pl.BlockSpec((2, EDGE, HEAD_DIM), lambda h: (0, 0, h))
    side = pl.BlockSpec((2, SIDE_PAD, HEAD_DIM), lambda h: (0, 0, h))
    bias = pl.BlockSpec((TILES, KEYS, TILE_Q), lambda h: (0, 0, 0))
    lse = pl.BlockSpec((1, 8, TILE_Q), lambda h: (h, 0, 0))
    mid = pl.BlockSpec((2, MID, HEAD_DIM), lambda h: (0, 0, h))
    return tokens, edge, side, bias, lse, mid


def forward_attention(q, k, v, halos, bias):
    tokens, edge, side, bias_spec, lse, _ = head_specs()
    return pl.pallas_call(
        forward_kernel,
        grid=(HEADS,),
        in_specs=[tokens, tokens, tokens, edge, edge, side, side, bias_spec],
        out_specs=[tokens, lse],
        out_shape=[
            jax.ShapeDtypeStruct((TOKENS, CHANNELS), BF16),
            jax.ShapeDtypeStruct((HEADS, 8, TILE_Q), F32),
        ],
        compiler_params=pltpu.CompilerParams(vmem_limit_bytes=32 * 1024 * 1024),
        cost_estimate=pl.CostEstimate(flops=2 * 10**9, bytes_accessed=8 * 10**6, transcendentals=10**6),
    )(q, k, v, *halos, bias)


def backward_attention(q, k, v, halos, bias, g, lse_array):
    tokens, edge, side, bias_spec, lse, mid = head_specs()
    keys = MID + 2 * SIDE_PAD
    return pl.pallas_call(
        backward_kernel,
        grid=(HEADS,),
        in_specs=[tokens, tokens, tokens, edge, edge, side, side, bias_spec, tokens, lse],
        out_specs=[tokens, mid, side, side],
        out_shape=[
            jax.ShapeDtypeStruct((TOKENS, CHANNELS), BF16),
            jax.ShapeDtypeStruct((2, MID, CHANNELS), F32),
            jax.ShapeDtypeStruct((2, SIDE_PAD, CHANNELS), BF16),
            jax.ShapeDtypeStruct((2, SIDE_PAD, CHANNELS), BF16),
        ],
        scratch_shapes=[pltpu.VMEM((keys, TOKENS), BF16), pltpu.VMEM((keys, TOKENS), BF16)],
        compiler_params=pltpu.CompilerParams(vmem_limit_bytes=32 * 1024 * 1024),
        cost_estimate=pl.CostEstimate(flops=4 * 10**9, bytes_accessed=12 * 10**6, transcendentals=10**6),
    )(q, k, v, *halos, bias, g, lse_array)


def along_lat(block, by):
    count = lax.axis_size(LAT)
    return lax.ppermute(block, LAT, [(i, i + by) for i in range(count) if 0 <= i + by < count])


def along_lon(block, by):
    count = lax.axis_size(LON)
    return lax.ppermute(block, LON, [(i, (i + by) % count) for i in range(count)])


def swapped(block, axis, bit):
    return lax.ppermute(block, axis, [(i, i ^ bit) for i in range(lax.axis_size(axis))])


def strip(keys, values, rows, cols):
    return jnp.stack([keys[rows, cols], values[rows, cols]]).reshape(2, -1, CHANNELS)


def halos_of(keys, values):
    every, first, last = slice(None), slice(0, REACH), slice(ROWS - REACH, ROWS)
    north = along_lat(strip(keys, values, last, every), 1)
    south = along_lat(strip(keys, values, first, every), -1)
    west = along_lon(strip(keys, values, every, last), 1)
    east = along_lon(strip(keys, values, every, first), -1)
    poles = jnp.stack([north, south], axis=1).reshape(2, 2, REACH, COLS, CHANNELS)
    corner_west = along_lon(poles[:, :, :, COLS - REACH :].reshape(2, 2, -1, CHANNELS), 1)
    corner_east = along_lon(poles[:, :, :, :REACH].reshape(2, 2, -1, CHANNELS), -1)
    unused = jnp.zeros((2, SIDE_PAD - SIDE, CHANNELS), BF16)
    west = jnp.concatenate([corner_west[:, 0], west, corner_west[:, 1], unused], axis=1)
    east = jnp.concatenate([corner_east[:, 0], east, corner_east[:, 1], unused], axis=1)
    return north, south, west, east


def sum_of_weight_terms(attended, grad_rows):
    half = CHANNELS // 2
    core = lax.axis_index("core")

    def term(which):
        part = lax.dynamic_slice_in_dim(attended, which * half, half, axis=1)
        return dot(part, grad_rows, ((0,), (0,)))

    received = swapped(term(1 - core).astype(BF16), "core", 1)
    pair = (term(core) + received.astype(F32)).astype(BF16)
    group = lax.axis_size(PLANE)
    pieces = lax.all_to_all(
        pair.reshape(group, half // group, WIDTH), PLANE, split_axis=0, concat_axis=0, tiled=True
    )
    total = jnp.sum(pieces.astype(F32), axis=0)
    for bit in (1, 2, 4):
        mine = total.astype(BF16)
        total = mine.astype(F32) + swapped(mine, "z", bit).astype(F32)
    whole = lax.all_to_all(
        jnp.broadcast_to(total.astype(BF16)[None], (group, half // group, WIDTH)),
        PLANE, split_axis=0, concat_axis=0, tiled=True,
    ).reshape(half, WIDTH)
    other = swapped(whole, "core", 1)
    first = jnp.where(core == 0, whole, other)
    second = jnp.where(core == 0, other, whole)
    return jnp.concatenate([first, second], axis=0).astype(F32)


def local(queries, key_vectors, value_vectors, grad_output, out_weight):
    first_row = lax.axis_index(LAT) * ROWS
    halos = halos_of(key_vectors, value_vectors)
    bias = window_bias(first_row, ROWS * lax.axis_size(LAT))
    grad_rows = grad_output.reshape(TOKENS, WIDTH)
    grad_attn = dot(grad_rows, out_weight, ((1,), (1,))).astype(BF16)
    q = queries.reshape(TOKENS, CHANNELS)
    k = key_vectors.reshape(TOKENS, CHANNELS)
    v = value_vectors.reshape(TOKENS, CHANNELS)
    attended, lse = forward_attention(q, k, v, halos, bias)
    grad_weight = sum_of_weight_terms(attended, grad_rows)
    grad_q, mid, side_west, side_east = backward_attention(q, k, v, halos, bias, grad_attn, lse)

    from_east = along_lon(side_west, -1)[:, :SIDE].reshape(2, SPAN, REACH, CHANNELS).astype(F32)
    from_west = along_lon(side_east, 1)[:, :SIDE].reshape(2, SPAN, REACH, CHANNELS).astype(F32)
    none = jnp.zeros((), F32)
    wide = COLS - REACH
    mid = mid.reshape(2, SPAN, COLS, CHANNELS)
    mid = mid + lax.pad(from_west, none, [(0, 0, 0), (0, 0, 0), (0, wide, 0), (0, 0, 0)])
    mid = mid + lax.pad(from_east, none, [(0, 0, 0), (0, 0, 0), (wide, 0, 0), (0, 0, 0)])
    from_south = along_lat(mid[:, :REACH].astype(BF16), -1).astype(F32)
    from_north = along_lat(mid[:, SPAN - REACH :].astype(BF16), 1).astype(F32)
    inner = mid[:, REACH : SPAN - REACH]
    tall = ROWS - REACH
    inner = inner + lax.pad(from_north, none, [(0, 0, 0), (0, tall, 0), (0, 0, 0), (0, 0, 0)])
    inner = inner + lax.pad(from_south, none, [(0, 0, 0), (tall, 0, 0), (0, 0, 0), (0, 0, 0)])
    inner = inner.astype(BF16)
    return grad_q.reshape(queries.shape), inner[0], inner[1], grad_weight


def solution(mesh):
    fine = Mesh(mesh.devices.reshape(2, 4, 8, 2, 2), LAT + LON)
    spread = P(LAT, LON, None)
    return jax.shard_map(
        local,
        mesh=fine,
        in_specs=(spread, spread, spread, spread, P()),
        out_specs=(spread, spread, spread, P()),
        check_vma=False,
    )
```

```python
import jax
import jax.numpy as jnp
import numpy as np
from jax import lax
from jax.experimental import pallas as pl
from jax.experimental.pallas import tpu as pltpu
from jax.sharding import Mesh, PartitionSpec as P

HEADS = 6
HALF_HEADS = HEADS // 2
HEAD_DIM = 128
WIDTH = 1536
WIN = 13
REACH = 6
ROWS = 16
COLS = 16
CHANNELS = HEADS * HEAD_DIM
HALF = CHANNELS // 2
TOKENS = ROWS * COLS
EDGE = REACH * COLS
SPAN = ROWS + 2 * REACH
MID = SPAN * COLS
CORNER = 80
CORNER_TILE = 48
SIDE = EDGE + CORNER
TILES = 2
TILE_Q = TOKENS // TILES
MID_TILE = 320
SIDE_TILE = EDGE + CORNER_TILE
KEYS = MID_TILE + 2 * SIDE_TILE
MID_STARTS = (0, 128)
CORNER_STARTS = (0, CORNER - CORNER_TILE)
SCALE = HEAD_DIM ** -0.5
LAT = ("xl", "y")
LON = ("z", "xh", "core")
HALOS = 6
PLANE = ("xl", "y", "xh")
F32 = jnp.float32
BF16 = jnp.bfloat16
FULL = pltpu.CompilerParams(vmem_limit_bytes=60 * 1024 * 1024)
SMALL = pltpu.CompilerParams(vmem_limit_bytes=16 * 1024 * 1024)


def side_places():
    count = REACH * REACH
    own_rows, own_cols = np.divmod(np.arange(EDGE), REACH)
    rows, cols = np.divmod(np.arange(count), REACH)
    spare = np.zeros(CORNER - 2 * count, np.int64)
    return (
        np.concatenate([REACH + own_rows, rows, REACH + ROWS + rows, spare]),
        np.concatenate([own_cols, cols, cols, spare]),
        np.arange(SIDE) < EDGE + 2 * count,
    )


def key_places(core):
    mid_rows, mid_cols = np.divmod(np.arange(MID), COLS)
    side_rows, side_cols, used = side_places()
    west_cols = np.where(used, side_cols - REACH, 1000)
    east_cols = np.where(used, side_cols + COLS, 1000)
    chip_cols, next_cols = (east_cols, west_cols) if core == 0 else (west_cols, east_cols)
    rows, cols = [], []
    for mid, corner in zip(MID_STARTS, CORNER_STARTS):
        mids = np.arange(mid, mid + MID_TILE)
        sides = np.concatenate([np.arange(EDGE), EDGE + corner + np.arange(CORNER_TILE)])
        rows.append(np.concatenate([mid_rows[mids], side_rows[sides], side_rows[sides]]) - REACH)
        cols.append(np.concatenate([mid_cols[mids], chip_cols[sides], next_cols[sides]]))
    return np.stack(rows), np.stack(cols)


def window_bias(core, first_row, total_rows):
    (rows, cols), (_, other_cols) = key_places(0), key_places(1)
    cols = jnp.where(core == 0, cols, other_cols)
    query_rows, query_cols = np.divmod(np.arange(TOKENS).reshape(TILES, TILE_Q), COLS)
    start = jnp.clip(first_row + query_rows - REACH, 0, total_rows - WIN)[:, None, :]
    key_rows = (first_row + rows)[:, :, None]
    near = jnp.abs(cols[:, :, None] - query_cols[:, None, :]) <= REACH
    keep = (key_rows >= start) & (key_rows < start + WIN) & near
    return jnp.where(keep, 0.0, -1e30).astype(F32)


def sent_cols(core):
    return (COLS - REACH, 0) if core == 0 else (0, COLS - REACH)


def strip_picks():
    picks = np.zeros((2, 2 * EDGE, TOKENS), np.float32)
    rows, cols = np.divmod(np.arange(EDGE), REACH)
    for core in range(2):
        for slot, col in enumerate(sent_cols(core)):
            picks[core, slot * EDGE + np.arange(EDGE), rows * COLS + cols + col] = 1
    return picks


def corner_picks():
    count = REACH * REACH
    picks = np.zeros((2, 2 * CORNER, 2 * EDGE), np.float32)
    rows, cols = np.divmod(np.arange(count), REACH)
    for core in range(2):
        for slot, col in enumerate(sent_cols(core)):
            for pole in range(2):
                at = slot * CORNER + pole * count + np.arange(count)
                picks[core, at, pole * EDGE + rows * COLS + cols + col] = 1
    return picks


def dot(a, b, dims):
    return lax.dot_general(a, b, (dims, ((), ())), preferred_element_type=F32)


def with_picks(kernel, core, picks, arrays, in_specs, out_specs, out_shape, steps, bytes_accessed):
    picks = jnp.asarray(picks, BF16)
    own = pl.BlockSpec((None,) + picks.shape[1:], lambda h, at: (at[0], 0, 0))
    return pl.pallas_call(
        kernel,
        grid_spec=pltpu.PrefetchScalarGridSpec(
            num_scalar_prefetch=1, grid=(steps,), in_specs=[own] + in_specs, out_specs=out_specs
        ),
        out_shape=out_shape,
        compiler_params=FULL,
        cost_estimate=pl.CostEstimate(flops=10**9, bytes_accessed=bytes_accessed, transcendentals=0),
    )(core, picks, *arrays)


def strip_kernel(core_ref, picks_ref, k_ref, v_ref, north_ref, south_ref, chip_ref, next_ref):
    for slot, ref in enumerate((k_ref, v_ref)):
        north_ref[slot] = ref[TOKENS - EDGE :, :]
        south_ref[slot] = ref[:EDGE, :]
        picked = dot(picks_ref[...], ref[...], ((1,), (0,))).astype(BF16)
        chip_ref[slot] = picked[:EDGE]
        next_ref[slot] = picked[EDGE:]


def strips_of(core, k, v):
    return with_picks(
        strip_kernel, core, strip_picks(), (k, v),
        [by_heads((), TOKENS, HEADS)] * 2, [by_heads((2,), EDGE, HEADS)] * 4,
        [jax.ShapeDtypeStruct((2, EDGE, CHANNELS), BF16)] * 4, 1, 2 * 10**6,
    )


def corner_kernel(core_ref, picks_ref, north_ref, south_ref, chip_ref, next_ref):
    for slot in range(2):
        poles = jnp.concatenate([north_ref[slot], south_ref[slot]], axis=0)
        picked = dot(picks_ref[...], poles, ((1,), (0,))).astype(BF16)
        chip_ref[slot] = picked[:CORNER]
        next_ref[slot] = picked[CORNER:]


def corners_of(core, north, south):
    return with_picks(
        corner_kernel, core, corner_picks(), (north, south),
        [by_heads((2,), EDGE, HEADS)] * 2, [by_heads((2,), CORNER, HEADS)] * 2,
        [jax.ShapeDtypeStruct((2, CORNER, CHANNELS), BF16)] * 2, 1, 10**6,
    )


def tile_keys(tile, own, north, south, chip, beyond, chip_corner, beyond_corner):
    corner = slice(CORNER_STARTS[tile], CORNER_STARTS[tile] + CORNER_TILE)
    if tile == 0:
        mid = [north, own[: MID_TILE - EDGE]]
    else:
        mid = [own[TOKENS - (MID_TILE - EDGE) :], south]
    return jnp.concatenate(mid + [chip, chip_corner[corner], beyond, beyond_corner[corner]], axis=0)


def forward_kernel(q_ref, k_ref, v_ref, *refs):
    halo_refs, (bias_ref, out_ref, lse_ref) = refs[:HALOS], refs[HALOS:]
    keys = (k_ref[...], *(ref[0] for ref in halo_refs))
    values = (v_ref[...], *(ref[1] for ref in halo_refs))
    for tile in range(TILES):
        span = slice(tile * TILE_Q, (tile + 1) * TILE_Q)
        scores = dot(tile_keys(tile, *keys), q_ref[span, :], ((1,), (1,))) * SCALE + bias_ref[tile]
        top = jnp.max(scores, axis=0, keepdims=True)
        exponent = jnp.exp(scores - top)
        total = jnp.sum(exponent, axis=0, keepdims=True)
        prob = (exponent * (1.0 / total)).astype(BF16)
        out_ref[span, :] = dot(prob, tile_keys(tile, *values), ((0,), (0,))).astype(BF16)
        lse_ref[0, tile : tile + 1, :] = top + jnp.log(total)


def backward_kernel(q_ref, k_ref, v_ref, *refs):
    halo_refs, (bias_ref, g_ref, lse_ref) = refs[:HALOS], refs[HALOS : HALOS + 3]
    dq_ref, own_ref, poles_ref, dchip_ref, dnext_ref, prob_s, score_s = refs[HALOS + 3 :]

    @pl.when(pl.program_id(0) == 0)
    def _():
        prob_s[...] = jnp.zeros_like(prob_s)
        score_s[...] = jnp.zeros_like(score_s)

    keys = (k_ref[...], *(ref[0] for ref in halo_refs))
    values = (v_ref[...], *(ref[1] for ref in halo_refs))
    for tile in range(TILES):
        span = slice(tile * TILE_Q, (tile + 1) * TILE_Q)
        key_tile = tile_keys(tile, *keys)
        scores = dot(key_tile, q_ref[span, :], ((1,), (1,))) * SCALE + bias_ref[tile]
        prob = jnp.exp(scores - lse_ref[0, tile : tile + 1, :])
        grad_prob = dot(tile_keys(tile, *values), g_ref[span, :], ((1,), (1,)))
        delta = jnp.sum(prob * grad_prob, axis=0, keepdims=True)
        grad_score = (prob * (grad_prob - delta) * SCALE).astype(BF16)
        dq_ref[span, :] = dot(grad_score, key_tile, ((0,), (0,))).astype(BF16)
        mid, corner = MID_STARTS[tile], CORNER_STARTS[tile]
        for part, scratch in ((prob.astype(BF16), prob_s), (grad_score, score_s)):
            scratch[mid : mid + MID_TILE, span] = part[:MID_TILE]
            for at, low in ((MID, MID_TILE), (MID + SIDE, MID_TILE + SIDE_TILE)):
                scratch[at : at + EDGE, span] = part[low : low + EDGE]
                at = at + EDGE + corner
                scratch[at : at + CORNER_TILE, span] = part[low + EDGE : low + SIDE_TILE]
    for slot, scratch, other in ((0, score_s, q_ref), (1, prob_s, g_ref)):
        grads = dot(scratch[...], other[...], ((1,), (0,)))
        poles_ref[slot, :EDGE] = grads[:EDGE]
        own_ref[slot] = grads[EDGE : EDGE + TOKENS]
        poles_ref[slot, EDGE:] = grads[EDGE + TOKENS : MID]
        dchip_ref[slot] = grads[MID : MID + SIDE].astype(BF16)
        dnext_ref[slot] = grads[MID + SIDE :].astype(BF16)


def by_heads(lead, rows, heads=1):
    shape = lead + (rows, heads * HEAD_DIM)
    return pl.BlockSpec(shape, lambda h, *at: (0,) * (len(lead) + 1) + (h,))


def input_specs():
    tokens = by_heads((), TOKENS)
    halos = [by_heads((2,), EDGE)] * 4 + [by_heads((2,), CORNER)] * 2
    bias = pl.BlockSpec((TILES, KEYS, TILE_Q), lambda h: (0, 0, 0))
    return [tokens] * 3 + halos + [bias]


def lse_spec():
    return pl.BlockSpec((1, 8, TILE_Q), lambda h: (h, 0, 0))


def forward_attention(q, k, v, halos, bias):
    return pl.pallas_call(
        forward_kernel,
        grid=(HEADS,),
        in_specs=input_specs(),
        out_specs=[by_heads((), TOKENS), lse_spec()],
        out_shape=[
            jax.ShapeDtypeStruct((TOKENS, CHANNELS), BF16),
            jax.ShapeDtypeStruct((HEADS, 8, TILE_Q), F32),
        ],
        compiler_params=FULL,
        cost_estimate=pl.CostEstimate(flops=2 * 10**9, bytes_accessed=6 * 10**6, transcendentals=10**6),
    )(q, k, v, *halos, bias)


def backward_attention(q, k, v, halos, bias, g, lse):
    keys = MID + 2 * SIDE
    return pl.pallas_call(
        backward_kernel,
        grid=(HEADS,),
        in_specs=input_specs() + [by_heads((), TOKENS), lse_spec()],
        out_specs=[by_heads((), TOKENS)] + [by_heads((2,), rows) for rows in (TOKENS, 2 * EDGE, SIDE, SIDE)],
        out_shape=[
            jax.ShapeDtypeStruct((TOKENS, CHANNELS), BF16),
            jax.ShapeDtypeStruct((2, TOKENS, CHANNELS), F32),
            jax.ShapeDtypeStruct((2, 2 * EDGE, CHANNELS), F32),
            jax.ShapeDtypeStruct((2, SIDE, CHANNELS), BF16),
            jax.ShapeDtypeStruct((2, SIDE, CHANNELS), BF16),
        ],
        scratch_shapes=[pltpu.VMEM((keys, TOKENS), BF16), pltpu.VMEM((keys, TOKENS), BF16)],
        compiler_params=FULL,
        cost_estimate=pl.CostEstimate(flops=6 * 10**9, bytes_accessed=12 * 10**6, transcendentals=10**6),
    )(q, k, v, *halos, bias, g, lse)


def merge_poles_kernel(core_ref, spread_ref, poles_ref, chip_ref, next_ref, north_ref, south_ref):
    for slot in range(2):
        corners = jnp.concatenate([chip_ref[slot, EDGE:], next_ref[slot, EDGE:]], axis=0)
        poles = (poles_ref[slot] + dot(spread_ref[...], corners, ((1,), (0,)))).astype(BF16)
        north_ref[slot] = poles[:EDGE]
        south_ref[slot] = poles[EDGE:]


def merge_poles(core, poles, from_chip, from_next):
    heads = 3
    return with_picks(
        merge_poles_kernel, core, corner_picks().transpose(0, 2, 1), (poles, from_chip, from_next),
        [by_heads((2,), rows, heads) for rows in (2 * EDGE, SIDE, SIDE)], [by_heads((2,), EDGE, heads)] * 2,
        [jax.ShapeDtypeStruct((2, EDGE, CHANNELS), BF16)] * 2, HEADS // heads, 4 * 10**6,
    )


def merge_own_kernel(
    core_ref, spread_ref, own_ref, chip_ref, next_ref, from_north_ref, from_south_ref, dk_ref, dv_ref
):
    low, high = EDGE, TOKENS - EDGE
    for slot, out_ref in enumerate((dk_ref, dv_ref)):
        sides = jnp.concatenate([chip_ref[slot, :EDGE], next_ref[slot, :EDGE]], axis=0)
        own = own_ref[slot] + dot(spread_ref[...], sides, ((1,), (0,)))
        out_ref[:low, :] = (own[:low] + from_north_ref[slot].astype(F32)).astype(BF16)
        out_ref[low:high, :] = own[low:high].astype(BF16)
        out_ref[high:, :] = (own[high:] + from_south_ref[slot].astype(F32)).astype(BF16)


def merge_own(core, own, from_chip, from_next, from_north, from_south):
    heads = 3
    return with_picks(
        merge_own_kernel, core, strip_picks().transpose(0, 2, 1), (own, from_chip, from_next, from_north, from_south),
        [by_heads((2,), rows, heads) for rows in (TOKENS, SIDE, SIDE, EDGE, EDGE)], [by_heads((), TOKENS, heads)] * 2,
        [jax.ShapeDtypeStruct((TOKENS, CHANNELS), BF16)] * 2, HEADS // heads, 6 * 10**6,
    )


def widen_kernel(which_ref, half_ref, *refs):
    refs[-1][...] = half_ref[...].astype(F32)


def widen_half(half, which, earlier=None):
    block = (HEAD_DIM, WIDTH)
    rest = [] if earlier is None else [earlier]
    return pl.pallas_call(
        widen_kernel,
        grid_spec=pltpu.PrefetchScalarGridSpec(
            num_scalar_prefetch=1,
            grid=(HALF_HEADS,),
            in_specs=[pl.BlockSpec(block, lambda h, at: (h, 0))] + [pl.BlockSpec(memory_space=pl.ANY)] * len(rest),
            out_specs=pl.BlockSpec(block, lambda h, at: (at[0] * HALF_HEADS + h, 0)),
        ),
        out_shape=jax.ShapeDtypeStruct((CHANNELS, WIDTH), F32),
        input_output_aliases={2: 0} if rest else {},
        compiler_params=SMALL,
        cost_estimate=pl.CostEstimate(flops=10**6, bytes_accessed=4 * 10**6, transcendentals=0),
    )(which, half, *rest)


def along_lat(block, by):
    bands = lax.axis_size(LAT)
    return lax.ppermute(block, LAT, [(i, i + by) for i in range(bands) if 0 <= i + by < bands])


def with_next_chip(block):
    strips = lax.axis_size(LON)
    return lax.ppermute(block, LON, [(j, (j + 2 * (j % 2) - 1) % strips) for j in range(strips)])


def swapped(block, axis, bit):
    return lax.ppermute(block, axis, [(i, i ^ bit) for i in range(lax.axis_size(axis))])


def with_chip(block):
    return swapped(block, "core", 1)


def halos_of(core, k, v):
    north, south, chip, beyond = strips_of(core, k, v)
    north, south = along_lat(north, 1), along_lat(south, -1)
    chip, beyond = with_chip(chip), with_next_chip(beyond)
    chip_corner, beyond_corner = corners_of(core, north, south)
    return north, south, chip, beyond, with_chip(chip_corner), with_next_chip(beyond_corner)


def plane_sum(pair):
    group = lax.axis_size(PLANE)
    return lax.all_to_all(
        pair.reshape(group, HALF // group, WIDTH), PLANE, split_axis=0, concat_axis=0, tiled=True
    )


def local(queries, key_vectors, value_vectors, grad_output, out_weight):
    core = lax.axis_index("core").astype(jnp.int32)
    q = queries.reshape(TOKENS, CHANNELS)
    k = key_vectors.reshape(TOKENS, CHANNELS)
    v = value_vectors.reshape(TOKENS, CHANNELS)
    grad_rows = grad_output.reshape(TOKENS, WIDTH)
    which = core.reshape(1)
    halos = halos_of(which, k, v)
    bias = window_bias(core, lax.axis_index(LAT) * ROWS, ROWS * lax.axis_size(LAT))
    grad_attn = dot(grad_rows, out_weight, ((1,), (1,))).astype(BF16)

    attended, lse = forward_attention(q, k, v, halos, bias)

    def term(half):
        return dot(lax.dynamic_slice_in_dim(attended, half * HALF, HALF, axis=1), grad_rows, ((0,), (0,)))

    received = swapped(term(1 - core).astype(BF16), "core", 1)
    pieces = plane_sum((term(core) + received.astype(F32)).astype(BF16))
    grad_q, own, poles, side_chip, side_next = backward_attention(q, k, v, halos, bias, grad_attn, lse)
    from_chip, from_next = with_chip(side_chip), with_next_chip(side_next)

    def z_step(total, bit):
        part = total.astype(BF16)
        return part.astype(F32) + swapped(part, "z", bit).astype(F32)

    pieces, grad_q = lax.optimization_barrier((pieces, grad_q))
    total = jnp.sum(pieces.astype(F32), axis=0)
    total = z_step(total, 1)
    total, from_chip, from_next = lax.optimization_barrier((total, from_chip, from_next))
    north, south = merge_poles(which, poles, from_chip, from_next)
    total = z_step(z_step(total, 2), 4)
    total, north, south = lax.optimization_barrier((total, north, south))
    group = lax.axis_size(PLANE)
    part = jnp.broadcast_to(total.astype(BF16)[None], (group, HALF // group, WIDTH))
    whole = plane_sum(part).reshape(HALF, WIDTH)
    from_north, from_south = along_lat(south, 1), along_lat(north, -1)
    whole, from_north, from_south = lax.optimization_barrier((whole, from_north, from_south))
    grad_k, grad_v = merge_own(which, own, from_chip, from_next, from_north, from_south)
    other = swapped(whole, "core", 1)
    grad_weight = widen_half(whole, which)
    grad_weight = widen_half(other, 1 - which, grad_weight)
    shape = queries.shape
    return grad_q.reshape(shape), grad_k.reshape(shape), grad_v.reshape(shape), grad_weight


def solution(mesh):
    fine = Mesh(mesh.devices.reshape(2, 4, 8, 2, 2), LAT + LON)
    spread = P(LAT, LON, None)
    return jax.shard_map(
        local,
        mesh=fine,
        in_specs=(spread, spread, spread, spread, P()),
        out_specs=(spread, spread, spread, P()),
        check_vma=False,
    )
```

```python
import jax
import jax.numpy as jnp
import numpy as np
from jax import lax
from jax.experimental import pallas as pl
from jax.experimental.pallas import tpu as pltpu
from jax.sharding import Mesh, PartitionSpec as P

HEADS = 6
HALF_HEADS = HEADS // 2
HEAD_DIM = 128
WIDTH = 1536
WIN = 13
REACH = 6
ROWS = 16
COLS = 16
CHANNELS = HEADS * HEAD_DIM
HALF = CHANNELS // 2
TOKENS = ROWS * COLS
EDGE = REACH * COLS
SPAN = ROWS + 2 * REACH
MID = SPAN * COLS
CORNER = 80
CORNER_TILE = 48
SIDE = EDGE + CORNER
TILES = 2
TILE_Q = TOKENS // TILES
MID_TILE = 320
SIDE_TILE = EDGE + CORNER_TILE
KEYS = MID_TILE + 2 * SIDE_TILE
MID_STARTS = (0, 128)
CORNER_STARTS = (0, CORNER - CORNER_TILE)
SCALE = HEAD_DIM ** -0.5
LAT = ("xl", "y")
LON = ("z", "xh", "core")
HALOS = 6
PLANE = ("xl", "y", "xh")
F32 = jnp.float32
BF16 = jnp.bfloat16
FULL = pltpu.CompilerParams(vmem_limit_bytes=60 * 1024 * 1024)
SMALL = pltpu.CompilerParams(vmem_limit_bytes=16 * 1024 * 1024)


def side_places():
    count = REACH * REACH
    own_rows, own_cols = np.divmod(np.arange(EDGE), REACH)
    rows, cols = np.divmod(np.arange(count), REACH)
    spare = np.zeros(CORNER - 2 * count, np.int64)
    return (
        np.concatenate([REACH + own_rows, rows, REACH + ROWS + rows, spare]),
        np.concatenate([own_cols, cols, cols, spare]),
        np.arange(SIDE) < EDGE + 2 * count,
    )


def key_places(core):
    mid_rows, mid_cols = np.divmod(np.arange(MID), COLS)
    side_rows, side_cols, used = side_places()
    west_cols = np.where(used, side_cols - REACH, 1000)
    east_cols = np.where(used, side_cols + COLS, 1000)
    chip_cols, next_cols = (east_cols, west_cols) if core == 0 else (west_cols, east_cols)
    rows, cols = [], []
    for mid, corner in zip(MID_STARTS, CORNER_STARTS):
        mids = np.arange(mid, mid + MID_TILE)
        sides = np.concatenate([np.arange(EDGE), EDGE + corner + np.arange(CORNER_TILE)])
        rows.append(np.concatenate([mid_rows[mids], side_rows[sides], side_rows[sides]]) - REACH)
        cols.append(np.concatenate([mid_cols[mids], chip_cols[sides], next_cols[sides]]))
    return np.stack(rows), np.stack(cols)


def window_bias(core, first_row, total_rows):
    (rows, cols), (_, other_cols) = key_places(0), key_places(1)
    cols = jnp.where(core == 0, cols, other_cols)
    query_rows, query_cols = np.divmod(np.arange(TOKENS).reshape(TILES, TILE_Q), COLS)
    start = jnp.clip(first_row + query_rows - REACH, 0, total_rows - WIN)[:, None, :]
    key_rows = (first_row + rows)[:, :, None]
    near = jnp.abs(cols[:, :, None] - query_cols[:, None, :]) <= REACH
    keep = (key_rows >= start) & (key_rows < start + WIN) & near
    return jnp.where(keep, 0.0, -1e30).astype(F32)


def sent_cols(core):
    return (COLS - REACH, 0) if core == 0 else (0, COLS - REACH)


def strip_picks():
    picks = np.zeros((2, 2 * EDGE, TOKENS), np.float32)
    rows, cols = np.divmod(np.arange(EDGE), REACH)
    for core in range(2):
        for slot, col in enumerate(sent_cols(core)):
            picks[core, slot * EDGE + np.arange(EDGE), rows * COLS + cols + col] = 1
    return picks


def corner_picks():
    count = REACH * REACH
    picks = np.zeros((2, 2 * CORNER, 2 * EDGE), np.float32)
    rows, cols = np.divmod(np.arange(count), REACH)
    for core in range(2):
        for slot, col in enumerate(sent_cols(core)):
            for pole in range(2):
                at = slot * CORNER + pole * count + np.arange(count)
                picks[core, at, pole * EDGE + rows * COLS + cols + col] = 1
    return picks


def dot(a, b, dims):
    return lax.dot_general(a, b, (dims, ((), ())), preferred_element_type=F32)


def with_picks(kernel, core, picks, arrays, in_specs, out_specs, out_shape, steps, bytes_accessed):
    picks = jnp.asarray(picks, BF16)
    own = pl.BlockSpec((None,) + picks.shape[1:], lambda h, at: (at[0], 0, 0))
    return pl.pallas_call(
        kernel,
        grid_spec=pltpu.PrefetchScalarGridSpec(
            num_scalar_prefetch=1, grid=(steps,), in_specs=[own] + in_specs, out_specs=out_specs
        ),
        out_shape=out_shape,
        compiler_params=FULL,
        cost_estimate=pl.CostEstimate(flops=10**9, bytes_accessed=bytes_accessed, transcendentals=0),
    )(core, picks, *arrays)


def strip_kernel(core_ref, picks_ref, k_ref, v_ref, north_ref, south_ref, chip_ref, next_ref):
    for slot, ref in enumerate((k_ref, v_ref)):
        north_ref[slot] = ref[TOKENS - EDGE :, :]
        south_ref[slot] = ref[:EDGE, :]
        picked = dot(picks_ref[...], ref[...], ((1,), (0,))).astype(BF16)
        chip_ref[slot] = picked[:EDGE]
        next_ref[slot] = picked[EDGE:]


def strips_of(core, k, v):
    return with_picks(
        strip_kernel, core, strip_picks(), (k, v),
        [by_heads((), TOKENS, HEADS)] * 2, [by_heads((2,), EDGE, HEADS)] * 4,
        [jax.ShapeDtypeStruct((2, EDGE, CHANNELS), BF16)] * 4, 1, 2 * 10**6,
    )


def corner_kernel(core_ref, picks_ref, north_ref, south_ref, chip_ref, next_ref):
    for slot in range(2):
        poles = jnp.concatenate([north_ref[slot], south_ref[slot]], axis=0)
        picked = dot(picks_ref[...], poles, ((1,), (0,))).astype(BF16)
        chip_ref[slot] = picked[:CORNER]
        next_ref[slot] = picked[CORNER:]


def corners_of(core, north, south):
    return with_picks(
        corner_kernel, core, corner_picks(), (north, south),
        [by_heads((2,), EDGE, HEADS)] * 2, [by_heads((2,), CORNER, HEADS)] * 2,
        [jax.ShapeDtypeStruct((2, CORNER, CHANNELS), BF16)] * 2, 1, 10**6,
    )


def tile_keys(tile, own, north, south, chip, beyond, chip_corner, beyond_corner):
    corner = slice(CORNER_STARTS[tile], CORNER_STARTS[tile] + CORNER_TILE)
    if tile == 0:
        mid = [north, own[: MID_TILE - EDGE]]
    else:
        mid = [own[TOKENS - (MID_TILE - EDGE) :], south]
    return jnp.concatenate(mid + [chip, chip_corner[corner], beyond, beyond_corner[corner]], axis=0)


def forward_kernel(base_ref, q_ref, k_ref, v_ref, *refs):
    halo_refs, (bias_ref, out_ref, lse_ref) = refs[:HALOS], refs[HALOS:]
    keys = (k_ref[...], *(ref[0] for ref in halo_refs))
    values = (v_ref[...], *(ref[1] for ref in halo_refs))
    for tile in range(TILES):
        span = slice(tile * TILE_Q, (tile + 1) * TILE_Q)
        scores = dot(tile_keys(tile, *keys), q_ref[span, :], ((1,), (1,))) * SCALE + bias_ref[tile]
        top = jnp.max(scores, axis=0, keepdims=True)
        exponent = jnp.exp(scores - top)
        total = jnp.sum(exponent, axis=0, keepdims=True)
        prob = (exponent * (1.0 / total)).astype(BF16)
        out_ref[span, :] = dot(prob, tile_keys(tile, *values), ((0,), (0,))).astype(BF16)
        lse_ref[0, tile : tile + 1, :] = top + jnp.log(total)


def backward_kernel(shift_ref, q_ref, k_ref, v_ref, *refs):
    halo_refs, (bias_ref, g_ref, lse_ref) = refs[:HALOS], refs[HALOS : HALOS + 3]
    dq_ref, own_ref, poles_ref, dchip_ref, dnext_ref, prob_s, score_s = refs[HALOS + 3 :]

    @pl.when(pl.program_id(0) == 0)
    def _():
        prob_s[...] = jnp.zeros_like(prob_s)
        score_s[...] = jnp.zeros_like(score_s)

    keys = (k_ref[...], *(ref[0] for ref in halo_refs))
    values = (v_ref[...], *(ref[1] for ref in halo_refs))
    for tile in range(TILES):
        span = slice(tile * TILE_Q, (tile + 1) * TILE_Q)
        key_tile = tile_keys(tile, *keys)
        scores = dot(key_tile, q_ref[span, :], ((1,), (1,))) * SCALE + bias_ref[tile]
        prob = jnp.exp(scores - lse_ref[0, tile : tile + 1, :])
        grad_prob = dot(tile_keys(tile, *values), g_ref[span, :], ((1,), (1,)))
        delta = jnp.sum(prob * grad_prob, axis=0, keepdims=True)
        grad_score = (prob * (grad_prob - delta) * SCALE).astype(BF16)
        dq_ref[span, :] = dot(grad_score, key_tile, ((0,), (0,))).astype(BF16)
        mid, corner = MID_STARTS[tile], CORNER_STARTS[tile]
        for part, scratch in ((prob.astype(BF16), prob_s), (grad_score, score_s)):
            scratch[mid : mid + MID_TILE, span] = part[:MID_TILE]
            for at, low in ((MID, MID_TILE), (MID + SIDE, MID_TILE + SIDE_TILE)):
                scratch[at : at + EDGE, span] = part[low : low + EDGE]
                at = at + EDGE + corner
                scratch[at : at + CORNER_TILE, span] = part[low + EDGE : low + SIDE_TILE]
    for slot, scratch, other in ((0, score_s, q_ref), (1, prob_s, g_ref)):
        grads = dot(scratch[...], other[...], ((1,), (0,)))
        poles_ref[slot, :EDGE] = grads[:EDGE]
        own_ref[slot] = grads[EDGE : EDGE + TOKENS]
        poles_ref[slot, EDGE:] = grads[EDGE + TOKENS : MID]
        dchip_ref[slot] = grads[MID : MID + SIDE].astype(BF16)
        dnext_ref[slot] = grads[MID + SIDE :].astype(BF16)


def by_heads(lead, rows, heads=1):
    shape = lead + (rows, heads * HEAD_DIM)
    return pl.BlockSpec(shape, lambda h, *at: (0,) * (len(lead) + 1) + (h,))


def from_head(lead, rows):
    return pl.BlockSpec(lead + (rows, HEAD_DIM), lambda h, at: (0,) * (len(lead) + 1) + (at[0] + h,))


def input_specs(head_spec):
    tokens = head_spec((), TOKENS)
    halos = [head_spec((2,), EDGE)] * 4 + [head_spec((2,), CORNER)] * 2
    bias = pl.BlockSpec((TILES, KEYS, TILE_Q), lambda h, *at: (0, 0, 0))
    return [tokens] * 3 + halos + [bias]


def forward_attention(base, q, k, v, halos, bias):
    return pl.pallas_call(
        forward_kernel,
        grid_spec=pltpu.PrefetchScalarGridSpec(
            num_scalar_prefetch=1,
            grid=(HALF_HEADS,),
            in_specs=input_specs(from_head),
            out_specs=[by_heads((), TOKENS), pl.BlockSpec((1, 8, TILE_Q), lambda h, at: (h, 0, 0))],
        ),
        out_shape=[
            jax.ShapeDtypeStruct((TOKENS, HALF), BF16),
            jax.ShapeDtypeStruct((HALF_HEADS, 8, TILE_Q), F32),
        ],
        compiler_params=FULL,
        cost_estimate=pl.CostEstimate(flops=2 * 10**9, bytes_accessed=6 * 10**6, transcendentals=10**6),
    )(base, q, k, v, *halos, bias)


def backward_attention(shift, q, k, v, halos, bias, g, lse):
    keys = MID + 2 * SIDE
    lse_spec = pl.BlockSpec((1, 8, TILE_Q), lambda h, at: (lax.rem(h + at[0], HEADS), 0, 0))
    return pl.pallas_call(
        backward_kernel,
        grid_spec=pltpu.PrefetchScalarGridSpec(
            num_scalar_prefetch=1,
            grid=(HEADS,),
            in_specs=input_specs(by_heads) + [by_heads((), TOKENS), lse_spec],
            out_specs=[by_heads((), TOKENS)] + [by_heads((2,), rows) for rows in (TOKENS, 2 * EDGE, SIDE, SIDE)],
            scratch_shapes=[pltpu.VMEM((keys, TOKENS), BF16), pltpu.VMEM((keys, TOKENS), BF16)],
        ),
        out_shape=[
            jax.ShapeDtypeStruct((TOKENS, CHANNELS), BF16),
            jax.ShapeDtypeStruct((2, TOKENS, CHANNELS), F32),
            jax.ShapeDtypeStruct((2, 2 * EDGE, CHANNELS), F32),
            jax.ShapeDtypeStruct((2, SIDE, CHANNELS), BF16),
            jax.ShapeDtypeStruct((2, SIDE, CHANNELS), BF16),
        ],
        compiler_params=FULL,
        cost_estimate=pl.CostEstimate(flops=6 * 10**9, bytes_accessed=12 * 10**6, transcendentals=10**6),
    )(shift, q, k, v, *halos, bias, g, lse)


def merge_poles_kernel(core_ref, spread_ref, poles_ref, chip_ref, next_ref, north_ref, south_ref):
    for slot in range(2):
        corners = jnp.concatenate([chip_ref[slot, EDGE:], next_ref[slot, EDGE:]], axis=0)
        poles = (poles_ref[slot] + dot(spread_ref[...], corners, ((1,), (0,)))).astype(BF16)
        north_ref[slot] = poles[:EDGE]
        south_ref[slot] = poles[EDGE:]


def merge_poles(core, poles, from_chip, from_next):
    heads = 3
    return with_picks(
        merge_poles_kernel, core, corner_picks().transpose(0, 2, 1), (poles, from_chip, from_next),
        [by_heads((2,), rows, heads) for rows in (2 * EDGE, SIDE, SIDE)], [by_heads((2,), EDGE, heads)] * 2,
        [jax.ShapeDtypeStruct((2, EDGE, CHANNELS), BF16)] * 2, HEADS // heads, 4 * 10**6,
    )


def merge_own_kernel(
    core_ref, spread_ref, own_ref, chip_ref, next_ref, from_north_ref, from_south_ref, dk_ref, dv_ref
):
    low, high = EDGE, TOKENS - EDGE
    for slot, out_ref in enumerate((dk_ref, dv_ref)):
        sides = jnp.concatenate([chip_ref[slot, :EDGE], next_ref[slot, :EDGE]], axis=0)
        own = own_ref[slot] + dot(spread_ref[...], sides, ((1,), (0,)))
        out_ref[:low, :] = (own[:low] + from_north_ref[slot].astype(F32)).astype(BF16)
        out_ref[low:high, :] = own[low:high].astype(BF16)
        out_ref[high:, :] = (own[high:] + from_south_ref[slot].astype(F32)).astype(BF16)


def merge_own(core, own, from_chip, from_next, from_north, from_south):
    heads = 3
    return with_picks(
        merge_own_kernel, core, strip_picks().transpose(0, 2, 1), (own, from_chip, from_next, from_north, from_south),
        [by_heads((2,), rows, heads) for rows in (TOKENS, SIDE, SIDE, EDGE, EDGE)], [by_heads((), TOKENS, heads)] * 2,
        [jax.ShapeDtypeStruct((TOKENS, CHANNELS), BF16)] * 2, HEADS // heads, 6 * 10**6,
    )


def widen_kernel(which_ref, half_ref, *refs):
    refs[-1][...] = half_ref[...].astype(F32)


def widen_half(half, which, earlier=None):
    block = (HEAD_DIM, WIDTH)
    rest = [] if earlier is None else [earlier]
    return pl.pallas_call(
        widen_kernel,
        grid_spec=pltpu.PrefetchScalarGridSpec(
            num_scalar_prefetch=1,
            grid=(HALF_HEADS,),
            in_specs=[pl.BlockSpec(block, lambda h, at: (h, 0))] + [pl.BlockSpec(memory_space=pl.ANY)] * len(rest),
            out_specs=pl.BlockSpec(block, lambda h, at: (at[0] * HALF_HEADS + h, 0)),
        ),
        out_shape=jax.ShapeDtypeStruct((CHANNELS, WIDTH), F32),
        input_output_aliases={2: 0} if rest else {},
        compiler_params=SMALL,
        cost_estimate=pl.CostEstimate(flops=10**6, bytes_accessed=4 * 10**6, transcendentals=0),
    )(which, half, *rest)


def along_lat(block, by):
    bands = lax.axis_size(LAT)
    return lax.ppermute(block, LAT, [(i, i + by) for i in range(bands) if 0 <= i + by < bands])


def with_next_chip(block):
    strips = lax.axis_size(LON)
    return lax.ppermute(block, LON, [(j, (j + 2 * (j % 2) - 1) % strips) for j in range(strips)])


def swapped(block, axis, bit):
    return lax.ppermute(block, axis, [(i, i ^ bit) for i in range(lax.axis_size(axis))])


def with_chip(block):
    return swapped(block, "core", 1)


def halos_of(core, k, v):
    north, south, chip, beyond = strips_of(core, k, v)
    north, south = along_lat(north, 1), along_lat(south, -1)
    chip, beyond = with_chip(chip), with_next_chip(beyond)
    chip_corner, beyond_corner = corners_of(core, north, south)
    return north, south, chip, beyond, with_chip(chip_corner), with_next_chip(beyond_corner)


def plane_sum(pair):
    group = lax.axis_size(PLANE)
    return lax.all_to_all(
        pair.reshape(group, HALF // group, WIDTH), PLANE, split_axis=0, concat_axis=0, tiled=True
    )


def local(queries, key_vectors, value_vectors, grad_output, out_weight):
    core = lax.axis_index("core").astype(jnp.int32)
    q = queries.reshape(TOKENS, CHANNELS)
    k = key_vectors.reshape(TOKENS, CHANNELS)
    v = value_vectors.reshape(TOKENS, CHANNELS)
    grad_rows = grad_output.reshape(TOKENS, WIDTH)
    which = core.reshape(1)
    halos = halos_of(which, k, v)
    bias = window_bias(core, lax.axis_index(LAT) * ROWS, ROWS * lax.axis_size(LAT))
    grad_attn = dot(grad_rows, out_weight, ((1,), (1,))).astype(BF16)

    theirs, lse_theirs = forward_attention(HALF_HEADS * (1 - which), q, k, v, halos, bias)
    received = with_chip(dot(theirs, grad_rows, ((0,), (0,))).astype(BF16))
    mine, lse_mine = forward_attention(HALF_HEADS * which, q, k, v, halos, bias)
    pieces = plane_sum((dot(mine, grad_rows, ((0,), (0,))) + received.astype(F32)).astype(BF16))
    grad_q, own, poles, side_chip, side_next = backward_attention(
        HALF_HEADS * (1 - which), q, k, v, halos, bias, grad_attn,
        jnp.concatenate([lse_theirs, lse_mine], axis=0),
    )
    from_chip, from_next = with_chip(side_chip), with_next_chip(side_next)

    pieces, grad_q = lax.optimization_barrier((pieces, grad_q))
    total = jnp.sum(pieces.astype(F32), axis=0)
    part = total.astype(BF16)
    near, far, last = (swapped(part, "z", bit).astype(F32) for bit in (1, 2, 3))
    total = (part.astype(F32) + near) + (far + last)
    total, from_chip, from_next = lax.optimization_barrier((total, from_chip, from_next))
    north, south = merge_poles(which, poles, from_chip, from_next)
    part = total.astype(BF16)
    total = part.astype(F32) + swapped(part, "z", 4).astype(F32)
    total, north, south = lax.optimization_barrier((total, north, south))
    group = lax.axis_size(PLANE)
    part = jnp.broadcast_to(total.astype(BF16)[None], (group, HALF // group, WIDTH))
    whole = plane_sum(part).reshape(HALF, WIDTH)
    from_north, from_south = along_lat(south, 1), along_lat(north, -1)
    grad_k, grad_v = merge_own(which, own, from_chip, from_next, from_north, from_south)
    whole, grad_k, grad_v = lax.optimization_barrier((whole, grad_k, grad_v))
    other = swapped(whole, "core", 1)
    grad_weight = widen_half(whole, which)
    grad_weight = widen_half(other, 1 - which, grad_weight)
    shape = queries.shape
    return grad_q.reshape(shape), grad_k.reshape(shape), grad_v.reshape(shape), grad_weight


def solution(mesh):
    fine = Mesh(mesh.devices.reshape(2, 4, 8, 2, 2), LAT + LON)
    spread = P(LAT, LON, None)
    return jax.shard_map(
        local,
        mesh=fine,
        in_specs=(spread, spread, spread, spread, P()),
        out_specs=(spread, spread, spread, P()),
        check_vma=False,
    )
```

```python
import jax
import jax.numpy as jnp
import numpy as np
from jax import lax
from jax.experimental import pallas as pl
from jax.experimental.pallas import tpu as pltpu
from jax.sharding import Mesh, PartitionSpec as P

HEADS = 6
HALF_HEADS = HEADS // 2
HEAD_DIM = 128
WIDTH = 1536
WIN = 13
REACH = 6
ROWS = 16
COLS = 16
CHANNELS = HEADS * HEAD_DIM
HALF = CHANNELS // 2
TOKENS = ROWS * COLS
EDGE = REACH * COLS
SPAN = ROWS + 2 * REACH
MID = SPAN * COLS
CORNER = 80
CORNER_TILE = 48
SIDE = EDGE + CORNER
TILES = 2
TILE_Q = TOKENS // TILES
MID_TILE = 320
SIDE_TILE = EDGE + CORNER_TILE
KEYS = MID_TILE + 2 * SIDE_TILE
MID_STARTS = (0, 128)
CORNER_STARTS = (0, CORNER - CORNER_TILE)
SCALE = HEAD_DIM ** -0.5
LAT = ("xl", "y")
LON = ("z", "xh", "core")
HALOS = 6
PLANE = ("xl", "y", "xh")
F32 = jnp.float32
BF16 = jnp.bfloat16
FULL = pltpu.CompilerParams(vmem_limit_bytes=60 * 1024 * 1024)
SMALL = pltpu.CompilerParams(vmem_limit_bytes=16 * 1024 * 1024)


def side_places():
    count = REACH * REACH
    own_rows, own_cols = np.divmod(np.arange(EDGE), REACH)
    rows, cols = np.divmod(np.arange(count), REACH)
    spare = np.zeros(CORNER - 2 * count, np.int64)
    return (
        np.concatenate([REACH + own_rows, rows, REACH + ROWS + rows, spare]),
        np.concatenate([own_cols, cols, cols, spare]),
        np.arange(SIDE) < EDGE + 2 * count,
    )


def key_places(core):
    mid_rows, mid_cols = np.divmod(np.arange(MID), COLS)
    side_rows, side_cols, used = side_places()
    west_cols = np.where(used, side_cols - REACH, 1000)
    east_cols = np.where(used, side_cols + COLS, 1000)
    chip_cols, next_cols = (east_cols, west_cols) if core == 0 else (west_cols, east_cols)
    rows, cols = [], []
    for mid, corner in zip(MID_STARTS, CORNER_STARTS):
        mids = np.arange(mid, mid + MID_TILE)
        sides = np.concatenate([np.arange(EDGE), EDGE + corner + np.arange(CORNER_TILE)])
        rows.append(np.concatenate([mid_rows[mids], side_rows[sides], side_rows[sides]]) - REACH)
        cols.append(np.concatenate([mid_cols[mids], chip_cols[sides], next_cols[sides]]))
    return np.stack(rows), np.stack(cols)


def window_bias(core, first_row, total_rows):
    (rows, cols), (_, other_cols) = key_places(0), key_places(1)
    cols = jnp.where(core == 0, cols, other_cols)
    query_rows, query_cols = np.divmod(np.arange(TOKENS).reshape(TILES, TILE_Q), COLS)
    start = jnp.clip(first_row + query_rows - REACH, 0, total_rows - WIN)[:, None, :]
    key_rows = (first_row + rows)[:, :, None]
    near = jnp.abs(cols[:, :, None] - query_cols[:, None, :]) <= REACH
    keep = (key_rows >= start) & (key_rows < start + WIN) & near
    return jnp.where(keep, 0.0, -1e30).astype(BF16)


def sent_cols(core):
    return (COLS - REACH, 0) if core == 0 else (0, COLS - REACH)


def strip_picks():
    picks = np.zeros((2, 2 * EDGE, TOKENS), np.float32)
    rows, cols = np.divmod(np.arange(EDGE), REACH)
    for core in range(2):
        for slot, col in enumerate(sent_cols(core)):
            picks[core, slot * EDGE + np.arange(EDGE), rows * COLS + cols + col] = 1
    return picks


def corner_picks():
    count = REACH * REACH
    picks = np.zeros((2, 2 * CORNER, 2 * EDGE), np.float32)
    rows, cols = np.divmod(np.arange(count), REACH)
    for core in range(2):
        for slot, col in enumerate(sent_cols(core)):
            for pole in range(2):
                at = slot * CORNER + pole * count + np.arange(count)
                picks[core, at, pole * EDGE + rows * COLS + cols + col] = 1
    return picks


def dot(a, b, dims):
    return lax.dot_general(a, b, (dims, ((), ())), preferred_element_type=F32)


def with_picks(kernel, core, picks, arrays, in_specs, out_specs, out_shape, steps, bytes_accessed):
    picks = jnp.asarray(picks, BF16)
    own = pl.BlockSpec((None,) + picks.shape[1:], lambda h, at: (at[0], 0, 0))
    return pl.pallas_call(
        kernel,
        grid_spec=pltpu.PrefetchScalarGridSpec(
            num_scalar_prefetch=1, grid=(steps,), in_specs=[own] + in_specs, out_specs=out_specs
        ),
        out_shape=out_shape,
        compiler_params=FULL,
        cost_estimate=pl.CostEstimate(flops=10**9, bytes_accessed=bytes_accessed, transcendentals=0),
    )(core, picks, *arrays)


def strip_kernel(core_ref, picks_ref, k_ref, v_ref, north_ref, south_ref, chip_ref, next_ref):
    for slot, ref in enumerate((k_ref, v_ref)):
        north_ref[slot] = ref[TOKENS - EDGE :, :]
        south_ref[slot] = ref[:EDGE, :]
        picked = dot(picks_ref[...], ref[...], ((1,), (0,))).astype(BF16)
        chip_ref[slot] = picked[:EDGE]
        next_ref[slot] = picked[EDGE:]


def strips_of(core, k, v):
    return with_picks(
        strip_kernel, core, strip_picks(), (k, v),
        [by_heads((), TOKENS, HEADS)] * 2, [by_heads((2,), EDGE, HEADS)] * 4,
        [jax.ShapeDtypeStruct((2, EDGE, CHANNELS), BF16)] * 4, 1, 2 * 10**6,
    )


def corner_kernel(core_ref, picks_ref, north_ref, south_ref, chip_ref, next_ref):
    for slot in range(2):
        poles = jnp.concatenate([north_ref[slot], south_ref[slot]], axis=0)
        picked = dot(picks_ref[...], poles, ((1,), (0,))).astype(BF16)
        chip_ref[slot] = picked[:CORNER]
        next_ref[slot] = picked[CORNER:]


def corners_of(core, north, south):
    return with_picks(
        corner_kernel, core, corner_picks(), (north, south),
        [by_heads((2,), EDGE, HEADS)] * 2, [by_heads((2,), CORNER, HEADS)] * 2,
        [jax.ShapeDtypeStruct((2, CORNER, CHANNELS), BF16)] * 2, 1, 10**6,
    )


def tile_keys(tile, own, north, south, chip, beyond, chip_corner, beyond_corner):
    corner = slice(CORNER_STARTS[tile], CORNER_STARTS[tile] + CORNER_TILE)
    if tile == 0:
        mid = [north, own[: MID_TILE - EDGE]]
    else:
        mid = [own[TOKENS - (MID_TILE - EDGE) :], south]
    return jnp.concatenate(mid + [chip, chip_corner[corner], beyond, beyond_corner[corner]], axis=0)


def forward_kernel(base_ref, q_ref, k_ref, v_ref, *refs):
    halo_refs, (bias_ref, out_ref, lse_ref) = refs[:HALOS], refs[HALOS:]
    keys = (k_ref[...], *(ref[0] for ref in halo_refs))
    values = (v_ref[...], *(ref[1] for ref in halo_refs))
    for tile in range(TILES):
        span = slice(tile * TILE_Q, (tile + 1) * TILE_Q)
        scores = dot(tile_keys(tile, *keys), q_ref[span, :], ((1,), (1,))) * SCALE + bias_ref[tile].astype(F32)
        top = jnp.max(scores, axis=0, keepdims=True)
        exponent = jnp.exp(scores - top)
        total = jnp.sum(exponent, axis=0, keepdims=True)
        prob = (exponent * (1.0 / total)).astype(BF16)
        out_ref[span, :] = dot(prob, tile_keys(tile, *values), ((0,), (0,))).astype(BF16)
        lse_ref[0, tile : tile + 1, :] = top + jnp.log(total)


def backward_kernel(shift_ref, q_ref, k_ref, v_ref, *refs):
    halo_refs, (bias_ref, g_ref, lse_ref) = refs[:HALOS], refs[HALOS : HALOS + 3]
    dq_ref, own_ref, poles_ref, dchip_ref, dnext_ref, prob_s, score_s = refs[HALOS + 3 :]

    @pl.when(pl.program_id(0) == 0)
    def _():
        prob_s[...] = jnp.zeros_like(prob_s)
        score_s[...] = jnp.zeros_like(score_s)

    keys = (k_ref[...], *(ref[0] for ref in halo_refs))
    values = (v_ref[...], *(ref[1] for ref in halo_refs))
    for tile in range(TILES):
        span = slice(tile * TILE_Q, (tile + 1) * TILE_Q)
        key_tile = tile_keys(tile, *keys)
        scores = dot(key_tile, q_ref[span, :], ((1,), (1,))) * SCALE + bias_ref[tile].astype(F32)
        prob = jnp.exp(scores - lse_ref[0, tile : tile + 1, :])
        grad_prob = dot(tile_keys(tile, *values), g_ref[span, :], ((1,), (1,)))
        delta = jnp.sum(prob * grad_prob, axis=0, keepdims=True)
        grad_score = (prob * (grad_prob - delta) * SCALE).astype(BF16)
        dq_ref[span, :] = dot(grad_score, key_tile, ((0,), (0,))).astype(BF16)
        mid, corner = MID_STARTS[tile], CORNER_STARTS[tile]
        for part, scratch in ((prob.astype(BF16), prob_s), (grad_score, score_s)):
            scratch[mid : mid + MID_TILE, span] = part[:MID_TILE]
            for at, low in ((MID, MID_TILE), (MID + SIDE, MID_TILE + SIDE_TILE)):
                scratch[at : at + EDGE, span] = part[low : low + EDGE]
                at = at + EDGE + corner
                scratch[at : at + CORNER_TILE, span] = part[low + EDGE : low + SIDE_TILE]
    for slot, scratch, other in ((0, score_s, q_ref), (1, prob_s, g_ref)):
        grads = dot(scratch[...], other[...], ((1,), (0,)))
        poles_ref[slot, :EDGE] = grads[:EDGE]
        own_ref[slot] = grads[EDGE : EDGE + TOKENS]
        poles_ref[slot, EDGE:] = grads[EDGE + TOKENS : MID]
        dchip_ref[slot] = grads[MID : MID + SIDE].astype(BF16)
        dnext_ref[slot] = grads[MID + SIDE :].astype(BF16)


def by_heads(lead, rows, heads=1):
    shape = lead + (rows, heads * HEAD_DIM)
    return pl.BlockSpec(shape, lambda h, *at: (0,) * (len(lead) + 1) + (h,))


def from_head(lead, rows):
    return pl.BlockSpec(lead + (rows, HEAD_DIM), lambda h, at: (0,) * (len(lead) + 1) + (at[0] + h,))


def input_specs(head_spec):
    tokens = head_spec((), TOKENS)
    halos = [head_spec((2,), EDGE)] * 4 + [head_spec((2,), CORNER)] * 2
    bias = pl.BlockSpec((TILES, KEYS, TILE_Q), lambda h, *at: (0, 0, 0))
    return [tokens] * 3 + halos + [bias]


def forward_attention(base, q, k, v, halos, bias):
    return pl.pallas_call(
        forward_kernel,
        grid_spec=pltpu.PrefetchScalarGridSpec(
            num_scalar_prefetch=1,
            grid=(HALF_HEADS,),
            in_specs=input_specs(from_head),
            out_specs=[by_heads((), TOKENS), pl.BlockSpec((1, 8, TILE_Q), lambda h, at: (h, 0, 0))],
        ),
        out_shape=[
            jax.ShapeDtypeStruct((TOKENS, HALF), BF16),
            jax.ShapeDtypeStruct((HALF_HEADS, 8, TILE_Q), F32),
        ],
        compiler_params=FULL,
        cost_estimate=pl.CostEstimate(flops=2 * 10**9, bytes_accessed=6 * 10**6, transcendentals=10**6),
    )(base, q, k, v, *halos, bias)


def backward_attention(shift, q, k, v, halos, bias, g, lse):
    keys = MID + 2 * SIDE
    lse_spec = pl.BlockSpec((1, 8, TILE_Q), lambda h, at: (lax.rem(h + at[0], HEADS), 0, 0))
    return pl.pallas_call(
        backward_kernel,
        grid_spec=pltpu.PrefetchScalarGridSpec(
            num_scalar_prefetch=1,
            grid=(HEADS,),
            in_specs=input_specs(by_heads) + [by_heads((), TOKENS), lse_spec],
            out_specs=[by_heads((), TOKENS)] + [by_heads((2,), rows) for rows in (TOKENS, 2 * EDGE, SIDE, SIDE)],
            scratch_shapes=[pltpu.VMEM((keys, TOKENS), BF16), pltpu.VMEM((keys, TOKENS), BF16)],
        ),
        out_shape=[
            jax.ShapeDtypeStruct((TOKENS, CHANNELS), BF16),
            jax.ShapeDtypeStruct((2, TOKENS, CHANNELS), F32),
            jax.ShapeDtypeStruct((2, 2 * EDGE, CHANNELS), F32),
            jax.ShapeDtypeStruct((2, SIDE, CHANNELS), BF16),
            jax.ShapeDtypeStruct((2, SIDE, CHANNELS), BF16),
        ],
        compiler_params=FULL,
        cost_estimate=pl.CostEstimate(flops=6 * 10**9, bytes_accessed=12 * 10**6, transcendentals=10**6),
    )(shift, q, k, v, *halos, bias, g, lse)


def merge_poles_kernel(core_ref, spread_ref, poles_ref, chip_ref, next_ref, north_ref, south_ref):
    for slot in range(2):
        corners = jnp.concatenate([chip_ref[slot, EDGE:], next_ref[slot, EDGE:]], axis=0)
        poles = (poles_ref[slot] + dot(spread_ref[...], corners, ((1,), (0,)))).astype(BF16)
        north_ref[slot] = poles[:EDGE]
        south_ref[slot] = poles[EDGE:]


def merge_poles(core, poles, from_chip, from_next):
    heads = 3
    return with_picks(
        merge_poles_kernel, core, corner_picks().transpose(0, 2, 1), (poles, from_chip, from_next),
        [by_heads((2,), rows, heads) for rows in (2 * EDGE, SIDE, SIDE)], [by_heads((2,), EDGE, heads)] * 2,
        [jax.ShapeDtypeStruct((2, EDGE, CHANNELS), BF16)] * 2, HEADS // heads, 4 * 10**6,
    )


def merge_own_kernel(
    core_ref, spread_ref, own_ref, chip_ref, next_ref, from_north_ref, from_south_ref, dk_ref, dv_ref
):
    low, high = EDGE, TOKENS - EDGE
    for slot, out_ref in enumerate((dk_ref, dv_ref)):
        sides = jnp.concatenate([chip_ref[slot, :EDGE], next_ref[slot, :EDGE]], axis=0)
        own = own_ref[slot] + dot(spread_ref[...], sides, ((1,), (0,)))
        out_ref[:low, :] = (own[:low] + from_north_ref[slot].astype(F32)).astype(BF16)
        out_ref[low:high, :] = own[low:high].astype(BF16)
        out_ref[high:, :] = (own[high:] + from_south_ref[slot].astype(F32)).astype(BF16)


def merge_own(core, own, from_chip, from_next, from_north, from_south):
    heads = 3
    return with_picks(
        merge_own_kernel, core, strip_picks().transpose(0, 2, 1), (own, from_chip, from_next, from_north, from_south),
        [by_heads((2,), rows, heads) for rows in (TOKENS, SIDE, SIDE, EDGE, EDGE)], [by_heads((), TOKENS, heads)] * 2,
        [jax.ShapeDtypeStruct((TOKENS, CHANNELS), BF16)] * 2, HEADS // heads, 6 * 10**6,
    )


def widen_kernel(which_ref, half_ref, *refs):
    refs[-1][...] = half_ref[...].astype(F32)


def widen_half(half, which, earlier=None):
    block = (HEAD_DIM, WIDTH)
    rest = [] if earlier is None else [earlier]
    return pl.pallas_call(
        widen_kernel,
        grid_spec=pltpu.PrefetchScalarGridSpec(
            num_scalar_prefetch=1,
            grid=(HALF_HEADS,),
            in_specs=[pl.BlockSpec(block, lambda h, at: (h, 0))] + [pl.BlockSpec(memory_space=pl.ANY)] * len(rest),
            out_specs=pl.BlockSpec(block, lambda h, at: (at[0] * HALF_HEADS + h, 0)),
        ),
        out_shape=jax.ShapeDtypeStruct((CHANNELS, WIDTH), F32),
        input_output_aliases={2: 0} if rest else {},
        compiler_params=SMALL,
        cost_estimate=pl.CostEstimate(flops=10**6, bytes_accessed=4 * 10**6, transcendentals=0),
    )(which, half, *rest)


def along_lat(block, by):
    bands = lax.axis_size(LAT)
    return lax.ppermute(block, LAT, [(i, i + by) for i in range(bands) if 0 <= i + by < bands])


def with_next_chip(block):
    strips = lax.axis_size(LON)
    return lax.ppermute(block, LON, [(j, (j + 2 * (j % 2) - 1) % strips) for j in range(strips)])


def swapped(block, axis, bit):
    return lax.ppermute(block, axis, [(i, i ^ bit) for i in range(lax.axis_size(axis))])


def with_chip(block):
    return swapped(block, "core", 1)


def halos_of(core, k, v):
    north, south, chip, beyond = strips_of(core, k, v)
    north, south = along_lat(north, 1), along_lat(south, -1)
    chip, beyond = with_chip(chip), with_next_chip(beyond)
    chip_corner, beyond_corner = corners_of(core, north, south)
    return north, south, chip, beyond, with_chip(chip_corner), with_next_chip(beyond_corner)


def plane_sum(pair):
    group = lax.axis_size(PLANE)
    return lax.all_to_all(
        pair.reshape(group, HALF // group, WIDTH), PLANE, split_axis=0, concat_axis=0, tiled=True
    )


def local(queries, key_vectors, value_vectors, grad_output, out_weight):
    core = lax.axis_index("core").astype(jnp.int32)
    q = queries.reshape(TOKENS, CHANNELS)
    k = key_vectors.reshape(TOKENS, CHANNELS)
    v = value_vectors.reshape(TOKENS, CHANNELS)
    grad_rows = grad_output.reshape(TOKENS, WIDTH)
    which = core.reshape(1)
    halos = halos_of(which, k, v)
    bias = window_bias(core, lax.axis_index(LAT) * ROWS, ROWS * lax.axis_size(LAT))
    grad_attn = dot(grad_rows, out_weight, ((1,), (1,))).astype(BF16)

    theirs, lse_theirs = forward_attention(HALF_HEADS * (1 - which), q, k, v, halos, bias)
    received = with_chip(dot(theirs, grad_rows, ((0,), (0,))).astype(BF16))
    mine, lse_mine = forward_attention(HALF_HEADS * which, q, k, v, halos, bias)
    pieces = plane_sum((dot(mine, grad_rows, ((0,), (0,))) + received.astype(F32)).astype(BF16))
    grad_q, own, poles, side_chip, side_next = backward_attention(
        HALF_HEADS * (1 - which), q, k, v, halos, bias, grad_attn,
        jnp.concatenate([lse_theirs, lse_mine], axis=0),
    )
    from_chip, from_next = with_chip(side_chip), with_next_chip(side_next)

    pieces, grad_q = lax.optimization_barrier((pieces, grad_q))
    total = jnp.sum(pieces.astype(F32), axis=0)
    part = total.astype(BF16)
    near, far, last = (swapped(part, "z", bit).astype(F32) for bit in (1, 2, 3))
    total = (part.astype(F32) + near) + (far + last)
    total, from_chip, from_next = lax.optimization_barrier((total, from_chip, from_next))
    north, south = merge_poles(which, poles, from_chip, from_next)
    part = total.astype(BF16)
    total = part.astype(F32) + swapped(part, "z", 4).astype(F32)
    total, north, south = lax.optimization_barrier((total, north, south))
    group = lax.axis_size(PLANE)
    part = jnp.broadcast_to(total.astype(BF16)[None], (group, HALF // group, WIDTH))
    whole = plane_sum(part).reshape(HALF, WIDTH)
    from_north, from_south = along_lat(south, 1), along_lat(north, -1)
    grad_k, grad_v = merge_own(which, own, from_chip, from_next, from_north, from_south)
    whole, grad_k, grad_v = lax.optimization_barrier((whole, grad_k, grad_v))
    other = swapped(whole, "core", 1)
    grad_weight = widen_half(whole, which)
    grad_weight = widen_half(other, 1 - which, grad_weight)
    shape = queries.shape
    return grad_q.reshape(shape), grad_k.reshape(shape), grad_v.reshape(shape), grad_weight


def solution(mesh):
    fine = Mesh(mesh.devices.reshape(2, 4, 8, 2, 2), LAT + LON)
    spread = P(LAT, LON, None)
    return jax.shard_map(
        local,
        mesh=fine,
        in_specs=(spread, spread, spread, spread, P()),
        out_specs=(spread, spread, spread, P()),
        check_vma=False,
    )
```
